32 devices in a mesh: grp: 8 (over y, x, core), blk: 4 (over z).
Axes of the slice: x: 2, y: 2, z: 4, core: 2. Of those that a mesh axis runs over, the one named last changes fastest.
Arguments:
- pixels: bfloat16 [32, 65536], P(None, ('grp', 'blk')), may hold values from -6 to 6
- landmark_index: int32 [1, 4096], P(None, ('grp', 'blk')), may hold values from 0 to 2047
- counts: int32 [1, 32], P(None, ('grp', 'blk')), may hold values from 64 to 128, as said below
- factor: bfloat16 [64, 4096], P(None, ('grp', 'blk')), may hold values from -6 to 6
Outputs:
- embedding: float32 [64, 65536], P(None, ('grp', 'blk'))
- log_degree: float32 [1, 65536], P(None, ('grp', 'blk'))
The draws below stay inside these ranges and needn't reach their ends.
Inputs may be any that keep to these rules, and one draw needn't show every extreme that they name: `landmark_index`: landmark slots of one device point at that device's own pixels. `counts`: some device has all 128 slots live in every draw.
All inputs are finite; a program needn't handle non-finite values.
Results may differ from the reference program's by a relative error of at most 0.0042.
Values may be sent and summed in bfloat16 or wider, within the bound.
A program may use at most 64 MiB of HBM per device.

```python
import jax
import jax.numpy as jnp
from jax import lax

LAYERS = 32
EMB = 64
PIX_DEV = 2048
CAP = 128
OWNERS = 32
PIXELS = 65536
LANDMARKS = 4096


def draw_counts(key, part):
    removed = jax.random.randint(key, (1, OWNERS), 0, CAP // 2 + 1)
    values = CAP - removed
    chosen = jax.random.randint(jax.random.fold_in(key, 1), (), 0, OWNERS)
    places = jnp.arange(OWNERS)[None, :]
    return jnp.where(places == chosen, CAP, values).astype(jnp.int32)


def place_ends(entries, key, least, top_value):
    dims = entries.shape
    place = [jax.random.randint(jax.random.fold_in(key, axis), (), 0, dims[axis]) for axis in range(len(dims))]
    entries = entries.at[tuple(place)].set(least)
    longest = dims.index(max(dims))
    place[longest] = (place[longest] + 1) % dims[longest]
    return entries.at[tuple(place)].set(top_value)


def steps_of(stream_key, dims, pieces, low, top_value):
    def one(axis_at, parts):
        heights = jax.random.uniform(jax.random.fold_in(jax.random.fold_in(stream_key, 6), axis_at), (parts,), jnp.float32, low / len(pieces), top_value / len(pieces))
        return jnp.repeat(jnp.exp(heights), dims[axis_at] // parts).reshape((-1,) + (1,) * (len(dims) - axis_at - 1))

    level = one(*pieces[0])
    for cut in pieces[1:]:
        level = level * one(*cut)
    return level


def normal_values(key, shape, width, most, shards=(), kind=jnp.bfloat16):
    level = steps_of(key, shape, shards, -0.22, 0.18) if shards else 1.0
    entries = jax.random.normal(key, shape, jnp.float32) * width * level
    return jnp.minimum(jnp.maximum(entries, -most), most).astype(kind)


def setup_inputs(seed: int = 0) -> dict:
    key_of = jax.random.split(jax.random.key(seed), 5)
    return {
        "pixels": normal_values(key_of[0], (LAYERS, PIXELS), 1.0, 6.0, ((1, 32),)),
        "landmark_index": place_ends(jax.random.randint(key_of[1], (1, LANDMARKS), 0, PIX_DEV), jax.random.fold_in(key_of[1], 1), 0, PIX_DEV - 1).astype(jnp.int32),
        "counts": draw_counts(jax.random.fold_in(key_of[4], 71), 0),
        "factor": normal_values(key_of[3], (EMB, LANDMARKS), 1.0, 6.0, ((1, 32),)),
    }


def reference(pixels, landmark_index, counts, factor):
    slots = jnp.arange(OWNERS * CAP, dtype=jnp.int32)
    owner = (slots // CAP).astype(jnp.int32)
    global_index = (landmark_index[0] + owner * PIX_DEV).astype(jnp.int32)
    land = jnp.take(pixels, global_index, axis=1)
    valid = slots % CAP < jnp.take(counts[0], owner)
    pix_sq = lax.optimization_barrier(jnp.sum(jnp.square(pixels.astype(jnp.float32)), axis=0, keepdims=True))
    land_blocks = jnp.transpose(land.reshape(LAYERS, OWNERS, CAP), (1, 0, 2))
    fac_blocks = jnp.transpose(factor.reshape(EMB, OWNERS, CAP), (1, 0, 2))
    mask_blocks = valid.reshape(OWNERS, CAP)

    def absorb(carry, inputs):
        emb_sum, deg_sum = carry
        land_blk, fac_blk, mask_blk = inputs
        cross = lax.dot_general(land_blk, pixels, (((0,), (0,)), ((), ())), preferred_element_type=jnp.float32)
        land_sq = lax.optimization_barrier(jnp.sum(jnp.square(land_blk.astype(jnp.float32)), axis=0))[:, None]
        dist = land_sq + pix_sq - 2.0 * cross
        kern = jnp.where(mask_blk[:, None], jnp.exp(-(2.0 / LAYERS) * dist), 0.0).astype(jnp.bfloat16)
        emb_sum = emb_sum + jnp.dot(fac_blk, kern, preferred_element_type=jnp.float32)
        deg_sum = deg_sum + lax.optimization_barrier(jnp.sum(kern.astype(jnp.float32), axis=0, keepdims=True))
        return ((emb_sum, deg_sum), None)
    start = (jnp.zeros((EMB, OWNERS * PIX_DEV), jnp.float32), jnp.zeros((1, OWNERS * PIX_DEV), jnp.float32))
    (raw_sum, degree), _ = lax.scan(absorb, start, (land_blocks, fac_blocks, mask_blocks))
    scaled = raw_sum * lax.rsqrt(degree)
    norms = jnp.sqrt(lax.optimization_barrier(jnp.mean(scaled * scaled, axis=1, keepdims=True)) + 1e-06)
    live = jnp.sum(counts.astype(jnp.float32))
    return (scaled / norms, jnp.log(degree / live))
```

```python
import functools

import jax
import jax.numpy as jnp
from jax import lax
from jax.experimental import pallas as pl
from jax.experimental.pallas import tpu as pltpu
from jax.sharding import PartitionSpec as P

MESH = pl.DeviceIdType.MESH
AUX = 16
CHUNK = 512


def three_way(value):
    high = value.astype(jnp.bfloat16)
    rest = value - high.astype(jnp.float32)
    mid = rest.astype(jnp.bfloat16)
    low = (rest - mid.astype(jnp.float32)).astype(jnp.bfloat16)
    return [part.astype(jnp.float32) for part in (high, mid, low)]


def kernel(
    groups, depth, counts_ref, index_ref, pixels_ref, factor_ref,
    scaled_ref, inv_ref, logdeg_ref,
    blocks, pix_aug, acc, rows_a, rows_b,
    recv_sem, z_sem, chip_sem, sib_sem, ra_send, ra_recv, rb_send, rb_recv,
):
    layers, pix = pixels_ref.shape
    emb, cap = factor_ref.shape
    chips = groups // 2
    g, z = lax.axis_index("grp"), lax.axis_index("blk")
    core, chip = lax.rem(g, 2), lax.div(g, 2)
    sib = g + 1 - 2 * core

    barrier = pltpu.get_barrier_semaphore()

    def greet_group(k, carry):
        pl.semaphore_signal(
            barrier, inc=1, device_id=(lax.rem(g + k, groups), z), device_id_type=MESH
        )
        return carry

    def greet_depth(k, carry):
        pl.semaphore_signal(
            barrier, inc=1, device_id=(g, lax.rem(z + k, depth)), device_id_type=MESH
        )
        return carry

    lax.fori_loop(1, groups, greet_group, 0)
    lax.fori_loop(1, depth, greet_depth, 0)

    pick = lax.broadcasted_iota(jnp.int32, (pix, cap), 0) == index_ref[...]
    land = jnp.dot(
        pixels_ref[...], pick.astype(jnp.bfloat16), preferred_element_type=jnp.float32
    )
    alive = lax.broadcasted_iota(jnp.int32, (1, cap), 1) < counts_ref[0, 0]
    land_sq = jnp.where(alive, jnp.sum(land * land, axis=0, keepdims=True) * (-0.0625), -1e30)
    row = lax.broadcasted_iota(jnp.int32, (AUX, cap), 0)
    aux = jnp.where(row < 3, 1.0, 0.0)
    for at, part in enumerate(three_way(land_sq)):
        aux = jnp.where(row == 3 + at, part, aux)
    mine = blocks.at[chip * depth + z, core]
    mine[0:emb, :] = factor_ref[...]
    mine[emb : emb + AUX, :] = aux.astype(jnp.bfloat16)
    mine[emb + AUX : emb + AUX + layers, :] = land.astype(jnp.bfloat16)

    pl.semaphore_wait(barrier, groups + depth - 2)

    def send(slot, which, device, send_sem):
        ref = blocks.at[slot, which]
        return pltpu.make_async_remote_copy(
            src_ref=ref, dst_ref=ref, send_sem=send_sem, recv_sem=recv_sem.at[slot, which],
            device_id=device, device_id_type=MESH,
        )

    def slot_of(dc, dz):
        return lax.rem(chip + dc, chips) * depth + lax.rem(z + dz, depth)

    def to_depth(dz):
        return send(slot_of(0, 0), core, (g, lax.rem(z + dz, depth)), z_sem.at[dz])

    def to_chip(dz, dc):
        there = lax.rem(chip + dc, chips) * 2 + core
        return send(slot_of(0, dz), core, (there, z), chip_sem.at[dz, dc])

    def to_sib(dc, dz):
        return send(slot_of(dc, dz), core, (sib, z), sib_sem.at[dc, dz])

    def arrived(slot, which):
        send(slot, which, (sib, z), sib_sem.at[0, 0]).wait_recv()

    to_sib(0, 0).start()
    for dz in range(1, depth):
        to_depth(dz).start()
    for dc in range(1, chips):
        to_chip(0, dc).start()

    for at in range(0, pix, CHUNK):
        cols = pl.ds(at, CHUNK)
        own = pixels_ref[:, cols].astype(jnp.float32)
        pix_sq = jnp.sum(own * own, axis=0, keepdims=True) * (-0.0625)
        prow = lax.broadcasted_iota(jnp.int32, (AUX, CHUNK), 0)
        side = jnp.where((prow >= 3) & (prow < 6), 1.0, 0.0)
        for put, part in enumerate(three_way(pix_sq)):
            side = jnp.where(prow == put, part, side)
        pix_aug[0:AUX, cols] = side.astype(jnp.bfloat16)
        pix_aug[AUX : AUX + layers, cols] = (own * 0.125).astype(jnp.bfloat16)
    acc[...] = jnp.zeros_like(acc)

    def absorb(slot):
        both = jnp.concatenate([blocks[slot, 0], blocks[slot, 1]], axis=1)
        fac = both[0 : emb + AUX]
        side = both[emb : emb + AUX + layers].astype(jnp.float32).T.astype(jnp.bfloat16)
        for at in range(0, pix, CHUNK):
            cols = pl.ds(at, CHUNK)
            expo = jnp.dot(side, pix_aug[:, cols], preferred_element_type=jnp.float32)
            kern = jnp.exp(expo).astype(jnp.bfloat16)
            acc[:, cols] += jnp.dot(fac, kern, preferred_element_type=jnp.float32)

    arrived(slot_of(0, 0), 1 - core)
    absorb(slot_of(0, 0))

    def relay(dz, carry):
        slot = slot_of(0, dz)
        arrived(slot, core)
        for dc in range(1, chips):
            to_chip(dz, dc).start()
        to_sib(0, dz).start()
        return carry

    lax.fori_loop(1, depth, relay, 0)

    def near(dc, carry):
        slot = slot_of(dc, 0)
        arrived(slot, core)
        to_sib(dc, 0).start()
        return carry

    lax.fori_loop(1, chips, near, 0)

    def column(dz, carry):
        slot = slot_of(0, dz)
        arrived(slot, 1 - core)
        absorb(slot)
        return carry

    lax.fori_loop(1, depth, column, 0)

    def rest(k, carry):
        dz, dc = lax.div(k, chips - 1), 1 + lax.rem(k, chips - 1)

        @pl.when(k + chips - 1 < depth * (chips - 1))
        def _():
            slot = slot_of(dc, dz + 1)
            arrived(slot, core)
            to_sib(dc, dz + 1).start()

        slot = slot_of(dc, dz)
        arrived(slot, 1 - core)
        absorb(slot)
        return carry

    lax.fori_loop(0, depth * (chips - 1), rest, 0)

    part = jnp.zeros((emb, 128), jnp.float32)
    for at in range(0, pix, 128):
        cols = pl.ds(at, 128)
        scaled = acc[0:emb, cols] * lax.rsqrt(acc[emb : emb + 1, cols])
        scaled_ref[:, cols] = scaled
        part = part + scaled * scaled
    tall = jnp.concatenate([part, jnp.zeros((128 - emb, 128), jnp.float32)], axis=0)
    total = jnp.sum(tall.T, axis=0, keepdims=True)
    lane = lax.broadcasted_iota(jnp.int32, (1, 128), 1)
    total = jnp.where(lane == emb, counts_ref[0, 0].astype(jnp.float32), total)

    def exchange(total, rows, count, device_of, send_sems, recv_sems):
        rows[0] = total

        def give(k):
            return pltpu.make_async_remote_copy(
                src_ref=rows.at[0], dst_ref=rows.at[k],
                send_sem=send_sems.at[k], recv_sem=recv_sems.at[k],
                device_id=device_of(k), device_id_type=MESH,
            )

        for k in range(1, count):
            give(k).start()
        for k in range(1, count):
            give(k).wait_recv()
            total = total + rows[k]
        for k in range(1, count):
            give(k).wait_send()
        return total

    total = exchange(total, rows_a, groups, lambda k: (lax.rem(g + k, groups), z), ra_send, ra_recv)
    total = exchange(total, rows_b, depth, lambda k: (g, lax.rem(z + k, depth)), rb_send, rb_recv)

    live = total[:, emb : emb + 1]
    logdeg_ref[...] = jnp.log(acc[emb : emb + 1, :] / live)
    inv = lax.rsqrt(total / (pix * groups * depth) + 1e-06)
    inv_ref[...] = jnp.broadcast_to(inv, (128, 128)).T[0:emb]

    for dz in range(1, depth):
        to_depth(dz).wait_send()
    for dz in range(depth):
        for dc in range(1, chips):
            to_chip(dz, dc).wait_send()
    for dc in range(chips):
        for dz in range(depth):
            to_sib(dc, dz).wait_send()


def per_device(groups, depth, pixels, landmark_index, counts, factor):
    layers, pix = pixels.shape
    emb, cap = factor.shape
    chips = groups // 2
    vmem = pl.BlockSpec(memory_space=pltpu.VMEM)
    dma = pltpu.SemaphoreType.DMA
    scaled, inv, logdeg = pl.pallas_call(
        functools.partial(kernel, groups, depth),
        out_shape=(
            jax.ShapeDtypeStruct((emb, pix), jnp.float32),
            jax.ShapeDtypeStruct((emb, 128), jnp.float32),
            jax.ShapeDtypeStruct((1, pix), jnp.float32),
        ),
        in_specs=[pl.BlockSpec(memory_space=pltpu.SMEM), vmem, vmem, vmem],
        out_specs=(vmem, vmem, vmem),
        scratch_shapes=[
            pltpu.VMEM((chips * depth, 2, emb + AUX + layers, cap), jnp.bfloat16),
            pltpu.VMEM((AUX + layers, pix), jnp.bfloat16),
            pltpu.VMEM((emb + AUX, pix), jnp.float32),
            pltpu.VMEM((groups, 1, 128), jnp.float32),
            pltpu.VMEM((depth, 1, 128), jnp.float32),
            dma((chips * depth, 2)),
            dma((depth,)),
            dma((depth, chips)),
            dma((chips, depth)),
            dma((groups,)),
            dma((groups,)),
            dma((depth,)),
            dma((depth,)),
        ],
        compiler_params=pltpu.CompilerParams(
            collective_id=0, has_side_effects=True, vmem_limit_bytes=40 * 1024 * 1024
        ),
        cost_estimate=pl.CostEstimate(
            flops=2 * pix * cap * groups * depth * (emb + layers),
            bytes_accessed=4 * emb * pix,
            transcendentals=pix * cap * groups * depth,
        ),
    )(counts, landmark_index, pixels, factor)
    return (scaled * inv[:, 0:1], logdeg)


def solution(mesh):
    placed = P(None, ("grp", "blk"))
    return jax.shard_map(
        functools.partial(per_device, mesh.shape["grp"], mesh.shape["blk"]),
        mesh=mesh,
        in_specs=(placed,) * 4,
        out_specs=(placed, placed),
        check_vma=False,
    )
```

```python
import functools

import jax
import jax.numpy as jnp
from jax import lax
from jax.experimental import pallas as pl
from jax.experimental.pallas import tpu as pltpu
from jax.sharding import PartitionSpec as P

MESH = pl.DeviceIdType.MESH
AUX = 16
CHUNK = 256
TOGETHER = 3
OUT = 512


def three_way(value):
    high = value.astype(jnp.bfloat16)
    rest = value - high.astype(jnp.float32)
    mid = rest.astype(jnp.bfloat16)
    low = (rest - mid.astype(jnp.float32)).astype(jnp.bfloat16)
    return [part.astype(jnp.float32) for part in (high, mid, low)]


def kernel(
    groups, depth, pixels_in, index_in, counts_in, factor_in,
    scaled_ref, inv_ref, logdeg_ref,
    pixels_ref, index_ref, counts_ref, in_sem,
    blocks, pix_aug, acc, rows_a, rows_b,
    recv_sem, z_sem, chip_sem, sib_sem, ra_send, ra_recv, rb_send, rb_recv,
):
    layers, pix = pixels_in.shape
    emb, cap = factor_in.shape
    chips = groups // 2
    g, z = lax.axis_index("grp"), lax.axis_index("blk")
    core, chip = lax.rem(g, 2), lax.div(g, 2)
    sib = g + 1 - 2 * core
    mine = blocks.at[chip * depth + z, core]

    loads = [
        pltpu.make_async_copy(src, dst, in_sem.at[at])
        for at, (src, dst) in enumerate(
            [
                (pixels_in, pixels_ref),
                (index_in, index_ref),
                (counts_in, counts_ref),
                (factor_in, mine.at[0:emb, :]),
            ]
        )
    ]
    for load in loads:
        load.start()

    barrier = pltpu.get_barrier_semaphore()

    def greet_group(k, carry):
        pl.semaphore_signal(
            barrier, inc=1, device_id=(lax.rem(g + k, groups), z), device_id_type=MESH
        )
        return carry

    def greet_depth(k, carry):
        pl.semaphore_signal(
            barrier, inc=1, device_id=(g, lax.rem(z + k, depth)), device_id_type=MESH
        )
        return carry

    lax.fori_loop(1, groups, greet_group, 0)
    lax.fori_loop(1, depth, greet_depth, 0)

    for load in loads:
        load.wait()

    pick = lax.broadcasted_iota(jnp.int32, (pix, cap), 0) == index_ref[...]
    land = jnp.dot(
        pixels_ref[...], pick.astype(jnp.bfloat16), preferred_element_type=jnp.float32
    )
    alive = lax.broadcasted_iota(jnp.int32, (1, cap), 1) < counts_ref[...]
    land_sq = jnp.where(alive, jnp.sum(land * land, axis=0, keepdims=True) * (-0.0625), -1e30)
    row = lax.broadcasted_iota(jnp.int32, (AUX, cap), 0)
    aux = jnp.where(row < 3, 1.0, 0.0)
    for at, part in enumerate(three_way(land_sq)):
        aux = jnp.where(row == 3 + at, part, aux)
    mine[emb : emb + AUX, :] = aux.astype(jnp.bfloat16)
    mine[emb + AUX : emb + AUX + layers, :] = land.astype(jnp.bfloat16)

    pl.semaphore_wait(barrier, groups + depth - 2)

    def send(slot, which, device, send_sem):
        ref = blocks.at[slot, which]
        return pltpu.make_async_remote_copy(
            src_ref=ref, dst_ref=ref, send_sem=send_sem, recv_sem=recv_sem.at[slot, which],
            device_id=device, device_id_type=MESH,
        )

    def slot_of(dc, dz):
        return lax.rem(chip + dc, chips) * depth + lax.rem(z + dz, depth)

    def to_depth(dz):
        return send(slot_of(0, 0), core, (g, lax.rem(z + dz, depth)), z_sem.at[dz])

    def to_chip(dz, dc):
        there = lax.rem(chip + dc, chips) * 2 + core
        return send(slot_of(0, dz), core, (there, z), chip_sem.at[dz, dc])

    def to_sib(dc, dz):
        return send(slot_of(dc, dz), core, (sib, z), sib_sem.at[dc, dz])

    def arrived(slot, which):
        send(slot, which, (sib, z), sib_sem.at[0, 0]).wait_recv()

    to_sib(0, 0).start()
    for dz in range(1, depth):
        to_depth(dz).start()
    for dc in range(1, chips):
        to_chip(0, dc).start()

    for at in range(0, pix, CHUNK):
        cols = pl.ds(at, CHUNK)
        own = pixels_ref[:, cols].astype(jnp.float32)
        pix_sq = jnp.sum(own * own, axis=0, keepdims=True) * (-0.0625)
        prow = lax.broadcasted_iota(jnp.int32, (AUX, CHUNK), 0)
        side = jnp.where((prow >= 3) & (prow < 6), 1.0, 0.0)
        for put, part in enumerate(three_way(pix_sq)):
            side = jnp.where(prow == put, part, side)
        pix_aug[0:AUX, cols] = side.astype(jnp.bfloat16)
        pix_aug[AUX : AUX + layers, cols] = (own * 0.125).astype(jnp.bfloat16)
    acc[...] = jnp.zeros_like(acc)

    def absorb(*slots):
        fac = jnp.concatenate(
            [blocks[slot, half, 0 : emb + AUX] for slot in slots for half in range(2)], axis=1
        )
        side = jnp.concatenate(
            [
                blocks[slot, half, emb : emb + AUX + layers].astype(jnp.float32).T
                for slot in slots
                for half in range(2)
            ],
            axis=0,
        ).astype(jnp.bfloat16)
        for at in range(0, pix, CHUNK):
            cols = pl.ds(at, CHUNK)
            expo = jnp.dot(side, pix_aug[:, cols], preferred_element_type=jnp.float32)
            kern = jnp.exp(expo).astype(jnp.bfloat16)
            acc[:, cols] += jnp.dot(fac, kern, preferred_element_type=jnp.float32)

    def bunches(count):
        return [range(at, min(at + TOGETHER, count)) for at in range(1, count, TOGETHER)]

    arrived(slot_of(0, 0), 1 - core)
    absorb(slot_of(0, 0))

    def relay(dz, carry):
        slot = slot_of(0, dz)
        arrived(slot, core)
        for dc in range(1, chips):
            to_chip(dz, dc).start()
        to_sib(0, dz).start()
        return carry

    lax.fori_loop(1, depth, relay, 0)

    def near(dc, carry):
        slot = slot_of(dc, 0)
        arrived(slot, core)
        to_sib(dc, 0).start()
        return carry

    lax.fori_loop(1, chips, near, 0)

    for bunch in bunches(depth):
        for dz in bunch:
            arrived(slot_of(0, dz), 1 - core)
        absorb(*[slot_of(0, dz) for dz in bunch])

    def rest(dz, carry):
        @pl.when(dz + 1 < depth)
        def _():
            for dc in range(1, chips):
                arrived(slot_of(dc, dz + 1), core)
                to_sib(dc, dz + 1).start()

        for bunch in bunches(chips):
            for dc in bunch:
                arrived(slot_of(dc, dz), 1 - core)
            absorb(*[slot_of(dc, dz) for dc in bunch])
        return carry

    lax.fori_loop(0, depth, rest, 0)

    part = jnp.zeros((emb, 128), jnp.float32)
    for at in range(0, pix, 128):
        cols = pl.ds(at, 128)
        scaled = acc[0:emb, cols] * lax.rsqrt(acc[emb : emb + 1, cols])
        scaled_ref[:, cols] = scaled
        part = part + scaled * scaled
    tall = jnp.concatenate([part, jnp.zeros((128 - emb, 128), jnp.float32)], axis=0)
    total = jnp.sum(tall.T, axis=0, keepdims=True)
    lane = lax.broadcasted_iota(jnp.int32, (1, 128), 1)
    total = jnp.where(lane == emb, counts_ref[...].astype(jnp.float32), total)

    def exchange(total, rows, count, device_of, send_sems, recv_sems):
        rows[0] = total

        def give(k):
            return pltpu.make_async_remote_copy(
                src_ref=rows.at[0], dst_ref=rows.at[k],
                send_sem=send_sems.at[k], recv_sem=recv_sems.at[k],
                device_id=device_of(k), device_id_type=MESH,
            )

        for k in range(1, count):
            give(k).start()
        for k in range(1, count):
            give(k).wait_recv()
            total = total + rows[k]
        for k in range(1, count):
            give(k).wait_send()
        return total

    total = exchange(total, rows_a, groups, lambda k: (lax.rem(g + k, groups), z), ra_send, ra_recv)
    total = exchange(total, rows_b, depth, lambda k: (g, lax.rem(z + k, depth)), rb_send, rb_recv)

    live = total[:, emb : emb + 1]
    logdeg_ref[...] = jnp.log(acc[emb : emb + 1, :] / live)
    inv = lax.rsqrt(total / (pix * groups * depth) + 1e-06)
    inv_ref[...] = jnp.broadcast_to(inv, (128, 128)).T[0:emb]

    for dz in range(1, depth):
        to_depth(dz).wait_send()
    for dz in range(depth):
        for dc in range(1, chips):
            to_chip(dz, dc).wait_send()
    for dc in range(chips):
        for dz in range(depth):
            to_sib(dc, dz).wait_send()


def finish(scaled_ref, inv_ref, logdeg_ref, emb_out, logdeg_out, held, sems):
    pix = scaled_ref.shape[1]
    copies = [pltpu.make_async_copy(logdeg_ref, logdeg_out, sems.at[pix // OUT])]
    copies[0].start()
    inv = inv_ref[...]
    for step in range(pix // OUT):
        for at in range(step * OUT, (step + 1) * OUT, 128):
            cols = pl.ds(at, 128)
            held[:, cols] = scaled_ref[:, cols] * inv
        cols = pl.ds(step * OUT, OUT)
        copy = pltpu.make_async_copy(held.at[:, cols], emb_out.at[:, cols], sems.at[step])
        copy.start()
        copies.append(copy)
    for copy in copies:
        copy.wait()


def per_device(groups, depth, pixels, landmark_index, counts, factor):
    layers, pix = pixels.shape
    emb, cap = factor.shape
    chips = groups // 2
    vmem = pl.BlockSpec(memory_space=pltpu.VMEM)
    dma = pltpu.SemaphoreType.DMA
    scaled, inv, logdeg = pl.pallas_call(
        functools.partial(kernel, groups, depth),
        out_shape=(
            jax.ShapeDtypeStruct((emb, pix), jnp.float32),
            jax.ShapeDtypeStruct((emb, 128), jnp.float32),
            jax.ShapeDtypeStruct((1, pix), jnp.float32),
        ),
        in_specs=[pl.BlockSpec(memory_space=pltpu.HBM)] * 4,
        out_specs=(vmem, vmem, vmem),
        scratch_shapes=[
            pltpu.VMEM((layers, pix), jnp.bfloat16),
            pltpu.VMEM((1, cap), jnp.int32),
            pltpu.VMEM((1, 1), jnp.int32),
            dma((4,)),
            pltpu.VMEM((chips * depth, 2, emb + AUX + layers, cap), jnp.bfloat16),
            pltpu.VMEM((AUX + layers, pix), jnp.bfloat16),
            pltpu.VMEM((emb + AUX, pix), jnp.float32),
            pltpu.VMEM((groups, 1, 128), jnp.float32),
            pltpu.VMEM((depth, 1, 128), jnp.float32),
            dma((chips * depth, 2)),
            dma((depth,)),
            dma((depth, chips)),
            dma((chips, depth)),
            dma((groups,)),
            dma((groups,)),
            dma((depth,)),
            dma((depth,)),
        ],
        compiler_params=pltpu.CompilerParams(
            collective_id=0, has_side_effects=True, vmem_limit_bytes=40 * 1024 * 1024
        ),
        cost_estimate=pl.CostEstimate(
            flops=2 * pix * cap * groups * depth * (emb + layers),
            bytes_accessed=4 * emb * pix,
            transcendentals=pix * cap * groups * depth,
        ),
    )(pixels, landmark_index, counts, factor)
    anywhere = pl.BlockSpec(memory_space=pltpu.HBM)
    return pl.pallas_call(
        finish,
        out_shape=(
            jax.ShapeDtypeStruct((emb, pix), jnp.float32),
            jax.ShapeDtypeStruct((1, pix), jnp.float32),
        ),
        in_specs=[vmem, vmem, vmem],
        out_specs=(anywhere, anywhere),
        scratch_shapes=[pltpu.VMEM((emb, pix), jnp.float32), dma((pix // OUT + 1,))],
        cost_estimate=pl.CostEstimate(
            flops=emb * pix, bytes_accessed=8 * emb * pix, transcendentals=0
        ),
    )(scaled, inv, logdeg)


def solution(mesh):
    placed = P(None, ("grp", "blk"))
    return jax.shard_map(
        functools.partial(per_device, mesh.shape["grp"], mesh.shape["blk"]),
        mesh=mesh,
        in_specs=(placed,) * 4,
        out_specs=(placed, placed),
        check_vma=False,
    )
```

```python
import functools

import jax
import jax.numpy as jnp
from jax import lax
from jax.experimental import pallas as pl
from jax.experimental.pallas import tpu as pltpu
from jax.sharding import PartitionSpec as P

MESH = pl.DeviceIdType.MESH
AUX = 16
CHUNK = 256
TOGETHER = 3


def three_way(value):
    high = value.astype(jnp.bfloat16)
    rest = value - high.astype(jnp.float32)
    mid = rest.astype(jnp.bfloat16)
    low = (rest - mid.astype(jnp.float32)).astype(jnp.bfloat16)
    return [part.astype(jnp.float32) for part in (high, mid, low)]


def kernel(
    groups, depth, pixels_in, index_in, counts_in, factor_in,
    scaled_ref, inv_ref, logdeg_ref,
    pixels_ref, index_ref, counts_ref, in_sem, out_sem,
    blocks, pix_aug, acc, rows_a, rows_b,
    recv_sem, z_sem, chip_sem, sib_sem, ra_send, ra_recv, rb_send, rb_recv,
):
    layers, pix = pixels_in.shape
    emb, cap = factor_in.shape
    chips = groups // 2
    g, z = lax.axis_index("grp"), lax.axis_index("blk")
    core, chip = lax.rem(g, 2), lax.div(g, 2)
    sib = g + 1 - 2 * core
    mine = blocks.at[chip * depth + z, core]

    loads = [
        pltpu.make_async_copy(src, dst, in_sem.at[at])
        for at, (src, dst) in enumerate(
            [
                (pixels_in, pixels_ref),
                (index_in, index_ref),
                (counts_in, counts_ref),
                (factor_in, mine.at[0:emb, :]),
            ]
        )
    ]
    for load in loads:
        load.start()

    barrier = pltpu.get_barrier_semaphore()

    def greet_group(k, carry):
        pl.semaphore_signal(
            barrier, inc=1, device_id=(lax.rem(g + k, groups), z), device_id_type=MESH
        )
        return carry

    def greet_depth(k, carry):
        pl.semaphore_signal(
            barrier, inc=1, device_id=(g, lax.rem(z + k, depth)), device_id_type=MESH
        )
        return carry

    lax.fori_loop(1, groups, greet_group, 0)
    lax.fori_loop(1, depth, greet_depth, 0)

    for load in loads:
        load.wait()

    pick = lax.broadcasted_iota(jnp.int32, (pix, cap), 0) == index_ref[...]
    land = jnp.dot(
        pixels_ref[...], pick.astype(jnp.bfloat16), preferred_element_type=jnp.float32
    )
    alive = lax.broadcasted_iota(jnp.int32, (1, cap), 1) < counts_ref[...]
    land_sq = jnp.where(alive, jnp.sum(land * land, axis=0, keepdims=True) * (-0.0625), -1e30)
    row = lax.broadcasted_iota(jnp.int32, (AUX, cap), 0)
    aux = jnp.where(row < 3, 1.0, 0.0)
    for at, part in enumerate(three_way(land_sq)):
        aux = jnp.where(row == 3 + at, part, aux)
    mine[emb : emb + AUX, :] = aux.astype(jnp.bfloat16)
    mine[emb + AUX : emb + AUX + layers, :] = land.astype(jnp.bfloat16)

    pl.semaphore_wait(barrier, groups + depth - 2)

    def send(slot, which, device, send_sem):
        ref = blocks.at[slot, which]
        return pltpu.make_async_remote_copy(
            src_ref=ref, dst_ref=ref, send_sem=send_sem, recv_sem=recv_sem.at[slot, which],
            device_id=device, device_id_type=MESH,
        )

    def slot_of(dc, dz):
        return lax.rem(chip + dc, chips) * depth + lax.rem(z + dz, depth)

    def to_depth(dz):
        return send(slot_of(0, 0), core, (g, lax.rem(z + dz, depth)), z_sem.at[dz])

    def to_chip(dz, dc):
        there = lax.rem(chip + dc, chips) * 2 + core
        return send(slot_of(0, dz), core, (there, z), chip_sem.at[dz, dc])

    def to_sib(dc, dz):
        return send(slot_of(dc, dz), core, (sib, z), sib_sem.at[dc, dz])

    def arrived(slot, which):
        send(slot, which, (sib, z), sib_sem.at[0, 0]).wait_recv()

    to_sib(0, 0).start()
    for dz in range(1, depth):
        to_depth(dz).start()
    for dc in range(1, chips):
        to_chip(0, dc).start()

    for at in range(0, pix, CHUNK):
        cols = pl.ds(at, CHUNK)
        own = pixels_ref[:, cols].astype(jnp.float32)
        pix_sq = jnp.sum(own * own, axis=0, keepdims=True) * (-0.0625)
        prow = lax.broadcasted_iota(jnp.int32, (AUX, CHUNK), 0)
        side = jnp.where((prow >= 3) & (prow < 6), 1.0, 0.0)
        for put, part in enumerate(three_way(pix_sq)):
            side = jnp.where(prow == put, part, side)
        pix_aug[0:AUX, cols] = side.astype(jnp.bfloat16)
        pix_aug[AUX : AUX + layers, cols] = (own * 0.125).astype(jnp.bfloat16)
    acc[...] = jnp.zeros_like(acc)

    def absorb(*slots):
        fac = jnp.concatenate(
            [blocks[slot, half, 0 : emb + AUX] for slot in slots for half in range(2)], axis=1
        )
        side = jnp.concatenate(
            [
                blocks[slot, half, emb : emb + AUX + layers].astype(jnp.float32).T
                for slot in slots
                for half in range(2)
            ],
            axis=0,
        ).astype(jnp.bfloat16)

        def exponent(at):
            return jnp.dot(
                side, pix_aug[:, at : at + CHUNK], preferred_element_type=jnp.float32
            )

        ahead = exponent(0)
        for at in range(0, pix, CHUNK):
            expo = ahead
            if at + CHUNK < pix:
                ahead = exponent(at + CHUNK)
            kern = jnp.exp(expo).astype(jnp.bfloat16)
            acc[:, at : at + CHUNK] += jnp.dot(fac, kern, preferred_element_type=jnp.float32)

    def bunches(count):
        return [range(at, min(at + TOGETHER, count)) for at in range(1, count, TOGETHER)]

    arrived(slot_of(0, 0), 1 - core)
    absorb(slot_of(0, 0))

    def relay(dz, carry):
        slot = slot_of(0, dz)
        arrived(slot, core)
        for dc in range(1, chips):
            to_chip(dz, dc).start()
        to_sib(0, dz).start()
        return carry

    lax.fori_loop(1, depth, relay, 0)

    def near(dc, carry):
        slot = slot_of(dc, 0)
        arrived(slot, core)
        to_sib(dc, 0).start()
        return carry

    lax.fori_loop(1, chips, near, 0)

    for bunch in bunches(depth):
        for dz in bunch:
            arrived(slot_of(0, dz), 1 - core)
        absorb(*[slot_of(0, dz) for dz in bunch])

    def rest(dz, carry):
        @pl.when(dz + 1 < depth)
        def _():
            for dc in range(1, chips):
                arrived(slot_of(dc, dz + 1), core)
                to_sib(dc, dz + 1).start()

        for bunch in bunches(chips):
            for dc in bunch:
                arrived(slot_of(dc, dz), 1 - core)
            absorb(*[slot_of(dc, dz) for dc in bunch])
        return carry

    lax.fori_loop(0, depth, rest, 0)

    part = jnp.zeros((emb, 128), jnp.float32)
    for at in range(0, pix, 128):
        cols = pl.ds(at, 128)
        scaled = acc[0:emb, cols] * lax.rsqrt(acc[emb : emb + 1, cols])
        acc[0:emb, cols] = scaled
        part = part + scaled * scaled
    give_scaled = pltpu.make_async_copy(acc.at[0:emb, :], scaled_ref, out_sem)
    give_scaled.start()
    tall = jnp.concatenate([part, jnp.zeros((128 - emb, 128), jnp.float32)], axis=0)
    total = jnp.sum(tall.T, axis=0, keepdims=True)
    lane = lax.broadcasted_iota(jnp.int32, (1, 128), 1)
    total = jnp.where(lane == emb, counts_ref[...].astype(jnp.float32), total)

    def exchange(total, rows, count, device_of, send_sems, recv_sems):
        rows[0] = total

        def give(k):
            return pltpu.make_async_remote_copy(
                src_ref=rows.at[0], dst_ref=rows.at[k],
                send_sem=send_sems.at[k], recv_sem=recv_sems.at[k],
                device_id=device_of(k), device_id_type=MESH,
            )

        for k in range(1, count):
            give(k).start()
        for k in range(1, count):
            give(k).wait_recv()
            total = total + rows[k]
        for k in range(1, count):
            give(k).wait_send()
        return total

    total = exchange(total, rows_a, groups, lambda k: (lax.rem(g + k, groups), z), ra_send, ra_recv)
    total = exchange(total, rows_b, depth, lambda k: (g, lax.rem(z + k, depth)), rb_send, rb_recv)

    live = total[:, emb : emb + 1]
    logdeg_ref[...] = jnp.log(acc[emb : emb + 1, :] / live)
    inv = lax.rsqrt(total / (pix * groups * depth) + 1e-06)
    inv_ref[...] = jnp.broadcast_to(inv, (128, 128)).T[0:emb]

    give_scaled.wait()
    for dz in range(1, depth):
        to_depth(dz).wait_send()
    for dz in range(depth):
        for dc in range(1, chips):
            to_chip(dz, dc).wait_send()
    for dc in range(chips):
        for dz in range(depth):
            to_sib(dc, dz).wait_send()


def per_device(groups, depth, pixels, landmark_index, counts, factor):
    layers, pix = pixels.shape
    emb, cap = factor.shape
    chips = groups // 2
    vmem = pl.BlockSpec(memory_space=pltpu.VMEM)
    dma = pltpu.SemaphoreType.DMA
    scaled, inv, logdeg = pl.pallas_call(
        functools.partial(kernel, groups, depth),
        out_shape=(
            jax.ShapeDtypeStruct((emb, pix), jnp.float32),
            jax.ShapeDtypeStruct((emb, 128), jnp.float32),
            jax.ShapeDtypeStruct((1, pix), jnp.float32),
        ),
        in_specs=[pl.BlockSpec(memory_space=pltpu.HBM)] * 4,
        out_specs=(pl.BlockSpec(memory_space=pltpu.HBM), vmem, vmem),
        scratch_shapes=[
            pltpu.VMEM((layers, pix), jnp.bfloat16),
            pltpu.VMEM((1, cap), jnp.int32),
            pltpu.VMEM((1, 1), jnp.int32),
            dma((4,)),
            dma,
            pltpu.VMEM((chips * depth, 2, emb + AUX + layers, cap), jnp.bfloat16),
            pltpu.VMEM((AUX + layers, pix), jnp.bfloat16),
            pltpu.VMEM((emb + AUX, pix), jnp.float32),
            pltpu.VMEM((groups, 1, 128), jnp.float32),
            pltpu.VMEM((depth, 1, 128), jnp.float32),
            dma((chips * depth, 2)),
            dma((depth,)),
            dma((depth, chips)),
            dma((chips, depth)),
            dma((groups,)),
            dma((groups,)),
            dma((depth,)),
            dma((depth,)),
        ],
        compiler_params=pltpu.CompilerParams(
            collective_id=0, has_side_effects=True, vmem_limit_bytes=56 * 1024 * 1024
        ),
        cost_estimate=pl.CostEstimate(
            flops=2 * pix * cap * groups * depth * (emb + layers),
            bytes_accessed=4 * emb * pix,
            transcendentals=pix * cap * groups * depth,
        ),
    )(pixels, landmark_index, counts, factor)
    return (scaled * inv[:, 0:1], logdeg)


def solution(mesh):
    placed = P(None, ("grp", "blk"))
    return jax.shard_map(
        functools.partial(per_device, mesh.shape["grp"], mesh.shape["blk"]),
        mesh=mesh,
        in_specs=(placed,) * 4,
        out_specs=(placed, placed),
        check_vma=False,
    )
```

```python
import functools

import jax
import jax.numpy as jnp
from jax import lax
from jax.experimental import pallas as pl
from jax.experimental.pallas import tpu as pltpu
from jax.sharding import PartitionSpec as P

MESH = pl.DeviceIdType.MESH
AUX = 16
CHUNK = 256
TOGETHER = 3
GIVE = 512


def three_way(value):
    high = value.astype(jnp.bfloat16)
    rest = value - high.astype(jnp.float32)
    mid = rest.astype(jnp.bfloat16)
    low = (rest - mid.astype(jnp.float32)).astype(jnp.bfloat16)
    return [part.astype(jnp.float32) for part in (high, mid, low)]


def kernel(
    groups, depth, pixels_in, index_in, counts_in, factor_in,
    emb_ref, logdeg_ref,
    pixels_ref, index_ref, counts_ref, in_sem, out_sem,
    blocks, pix_aug, acc, rows_a, rows_b,
    recv_sem, z_sem, chip_sem, sib_sem, ra_send, ra_recv, rb_send, rb_recv,
):
    layers, pix = pixels_in.shape
    emb, cap = factor_in.shape
    chips = groups // 2
    g, z = lax.axis_index("grp"), lax.axis_index("blk")
    core, chip = lax.rem(g, 2), lax.div(g, 2)
    sib = g + 1 - 2 * core
    mine = blocks.at[chip * depth + z, core]

    loads = [
        pltpu.make_async_copy(src, dst, in_sem.at[at])
        for at, (src, dst) in enumerate(
            [
                (pixels_in, pixels_ref),
                (index_in, index_ref),
                (counts_in, counts_ref),
                (factor_in, mine.at[0:emb, :]),
            ]
        )
    ]
    for load in loads:
        load.start()

    barrier = pltpu.get_barrier_semaphore()

    def greet_group(k, carry):
        pl.semaphore_signal(
            barrier, inc=1, device_id=(lax.rem(g + k, groups), z), device_id_type=MESH
        )
        return carry

    def greet_depth(k, carry):
        pl.semaphore_signal(
            barrier, inc=1, device_id=(g, lax.rem(z + k, depth)), device_id_type=MESH
        )
        return carry

    lax.fori_loop(1, groups, greet_group, 0)
    lax.fori_loop(1, depth, greet_depth, 0)

    for load in loads:
        load.wait()

    pick = lax.broadcasted_iota(jnp.int32, (pix, cap), 0) == index_ref[...]
    land = jnp.dot(
        pixels_ref[...], pick.astype(jnp.bfloat16), preferred_element_type=jnp.float32
    )
    alive = lax.broadcasted_iota(jnp.int32, (1, cap), 1) < counts_ref[...]
    land_sq = jnp.where(alive, jnp.sum(land * land, axis=0, keepdims=True) * (-0.0625), -1e30)
    row = lax.broadcasted_iota(jnp.int32, (AUX, cap), 0)
    aux = jnp.where(row < 3, 1.0, 0.0)
    for at, part in enumerate(three_way(land_sq)):
        aux = jnp.where(row == 3 + at, part, aux)
    mine[emb : emb + AUX, :] = aux.astype(jnp.bfloat16)
    mine[emb + AUX : emb + AUX + layers, :] = land.astype(jnp.bfloat16)

    pl.semaphore_wait(barrier, groups + depth - 2)

    def send(slot, which, device, send_sem):
        ref = blocks.at[slot, which]
        return pltpu.make_async_remote_copy(
            src_ref=ref, dst_ref=ref, send_sem=send_sem, recv_sem=recv_sem.at[slot, which],
            device_id=device, device_id_type=MESH,
        )

    def slot_of(dc, dz):
        return lax.rem(chip + dc, chips) * depth + lax.rem(z + dz, depth)

    def to_depth(dz):
        return send(slot_of(0, 0), core, (g, lax.rem(z + dz, depth)), z_sem.at[dz])

    def to_chip(dz, dc):
        there = lax.rem(chip + dc, chips) * 2 + core
        return send(slot_of(0, dz), core, (there, z), chip_sem.at[dz, dc])

    def to_sib(dc, dz):
        return send(slot_of(dc, dz), core, (sib, z), sib_sem.at[dc, dz])

    def arrived(slot, which):
        send(slot, which, (sib, z), sib_sem.at[0, 0]).wait_recv()

    to_sib(0, 0).start()
    for dz in range(1, depth):
        to_depth(dz).start()
    for dc in range(1, chips):
        to_chip(0, dc).start()

    for at in range(0, pix, CHUNK):
        cols = pl.ds(at, CHUNK)
        own = pixels_ref[:, cols].astype(jnp.float32)
        pix_sq = jnp.sum(own * own, axis=0, keepdims=True) * (-0.0625)
        prow = lax.broadcasted_iota(jnp.int32, (AUX, CHUNK), 0)
        side = jnp.where((prow >= 3) & (prow < 6), 1.0, 0.0)
        for put, part in enumerate(three_way(pix_sq)):
            side = jnp.where(prow == put, part, side)
        pix_aug[0:AUX, cols] = side.astype(jnp.bfloat16)
        pix_aug[AUX : AUX + layers, cols] = (own * 0.125).astype(jnp.bfloat16)
    acc[...] = jnp.zeros_like(acc)

    def absorb(*slots):
        def both(slot, rows):
            return [blocks[slot, half, rows] for half in range(2)]

        facs = [jnp.concatenate(both(slot, slice(0, emb + AUX)), axis=1) for slot in slots]
        sides = [
            jnp.concatenate(
                [half.astype(jnp.float32).T for half in both(slot, slice(emb, emb + AUX + layers))],
                axis=0,
            ).astype(jnp.bfloat16)
            for slot in slots
        ]
        tiles = [(at, k) for at in range(0, pix, CHUNK) for k in range(len(slots))]

        def exponent(at, k):
            return jnp.dot(
                sides[k], pix_aug[:, at : at + CHUNK], preferred_element_type=jnp.float32
            )

        ahead = exponent(*tiles[0])
        total = None
        for turn, (at, k) in enumerate(tiles):
            expo = ahead
            if turn + 1 < len(tiles):
                ahead = exponent(*tiles[turn + 1])
            kern = jnp.exp(expo).astype(jnp.bfloat16)
            add = jnp.dot(facs[k], kern, preferred_element_type=jnp.float32)
            total = add if k == 0 else total + add
            if k + 1 == len(slots):
                acc[:, at : at + CHUNK] += total

    def bunches(count):
        return [range(at, min(at + TOGETHER, count)) for at in range(1, count, TOGETHER)]

    arrived(slot_of(0, 0), 1 - core)
    absorb(slot_of(0, 0))

    def relay(dz, carry):
        slot = slot_of(0, dz)
        arrived(slot, core)
        for dc in range(1, chips):
            to_chip(dz, dc).start()
        to_sib(0, dz).start()
        return carry

    lax.fori_loop(1, depth, relay, 0)

    def near(dc, carry):
        slot = slot_of(dc, 0)
        arrived(slot, core)
        to_sib(dc, 0).start()
        return carry

    lax.fori_loop(1, chips, near, 0)

    for bunch in bunches(depth):
        for dz in bunch:
            arrived(slot_of(0, dz), 1 - core)
        absorb(*[slot_of(0, dz) for dz in bunch])

    def rest(dz, carry):
        @pl.when(dz + 1 < depth)
        def _():
            for dc in range(1, chips):
                arrived(slot_of(dc, dz + 1), core)
                to_sib(dc, dz + 1).start()

        for bunch in bunches(chips):
            for dc in bunch:
                arrived(slot_of(dc, dz), 1 - core)
            absorb(*[slot_of(dc, dz) for dc in bunch])
        return carry

    lax.fori_loop(0, depth, rest, 0)

    part = jnp.zeros((emb, 128), jnp.float32)
    for at in range(0, pix, 128):
        cols = pl.ds(at, 128)
        scaled = acc[0:emb, cols] * lax.rsqrt(acc[emb : emb + 1, cols])
        acc[0:emb, cols] = scaled
        part = part + scaled * scaled
    tall = jnp.concatenate([part, jnp.zeros((128 - emb, 128), jnp.float32)], axis=0)
    total = jnp.sum(tall.T, axis=0, keepdims=True)
    lane = lax.broadcasted_iota(jnp.int32, (1, 128), 1)
    total = jnp.where(lane == emb, counts_ref[...].astype(jnp.float32), total)

    def exchange(total, rows, count, device_of, send_sems, recv_sems):
        rows[0] = total

        def give(k):
            return pltpu.make_async_remote_copy(
                src_ref=rows.at[0], dst_ref=rows.at[k],
                send_sem=send_sems.at[k], recv_sem=recv_sems.at[k],
                device_id=device_of(k), device_id_type=MESH,
            )

        for k in range(1, count):
            give(k).start()
        for k in range(1, count):
            give(k).wait_recv()
            total = total + rows[k]
        for k in range(1, count):
            give(k).wait_send()
        return total

    total = exchange(total, rows_a, groups, lambda k: (lax.rem(g + k, groups), z), ra_send, ra_recv)
    total = exchange(total, rows_b, depth, lambda k: (g, lax.rem(z + k, depth)), rb_send, rb_recv)

    inv = lax.rsqrt(total / (pix * groups * depth) + 1e-06)
    inv = jnp.broadcast_to(inv, (128, 128)).T[0:emb]
    gives = []
    for at in range(0, pix, GIVE):
        for col in range(at, at + GIVE, 128):
            acc[0:emb, col : col + 128] = acc[0:emb, col : col + 128] * inv
        part = pl.ds(at, GIVE)
        gives.append(
            pltpu.make_async_copy(acc.at[0:emb, part], emb_ref.at[:, part], out_sem.at[at // GIVE])
        )
        gives[-1].start()
    live = total[:, emb : emb + 1]
    logdeg_ref[...] = jnp.log(acc[emb : emb + 1, :] / live)
    for give in gives:
        give.wait()
    for dz in range(1, depth):
        to_depth(dz).wait_send()
    for dz in range(depth):
        for dc in range(1, chips):
            to_chip(dz, dc).wait_send()
    for dc in range(chips):
        for dz in range(depth):
            to_sib(dc, dz).wait_send()


def per_device(groups, depth, pixels, landmark_index, counts, factor):
    layers, pix = pixels.shape
    emb, cap = factor.shape
    chips = groups // 2
    vmem = pl.BlockSpec(memory_space=pltpu.VMEM)
    dma = pltpu.SemaphoreType.DMA
    return pl.pallas_call(
        functools.partial(kernel, groups, depth),
        out_shape=(
            jax.ShapeDtypeStruct((emb, pix), jnp.float32),
            jax.ShapeDtypeStruct((1, pix), jnp.float32),
        ),
        in_specs=[pl.BlockSpec(memory_space=pltpu.HBM)] * 4,
        out_specs=(pl.BlockSpec(memory_space=pltpu.HBM), vmem),
        scratch_shapes=[
            pltpu.VMEM((layers, pix), jnp.bfloat16),
            pltpu.VMEM((1, cap), jnp.int32),
            pltpu.VMEM((1, 1), jnp.int32),
            dma((4,)),
            dma((pix // GIVE,)),
            pltpu.VMEM((chips * depth, 2, emb + AUX + layers, cap), jnp.bfloat16),
            pltpu.VMEM((AUX + layers, pix), jnp.bfloat16),
            pltpu.VMEM((emb + AUX, pix), jnp.float32),
            pltpu.VMEM((groups, 1, 128), jnp.float32),
            pltpu.VMEM((depth, 1, 128), jnp.float32),
            dma((chips * depth, 2)),
            dma((depth,)),
            dma((depth, chips)),
            dma((chips, depth)),
            dma((groups,)),
            dma((groups,)),
            dma((depth,)),
            dma((depth,)),
        ],
        compiler_params=pltpu.CompilerParams(
            collective_id=0, has_side_effects=True, vmem_limit_bytes=56 * 1024 * 1024
        ),
        cost_estimate=pl.CostEstimate(
            flops=2 * pix * cap * groups * depth * (emb + layers),
            bytes_accessed=4 * emb * pix,
            transcendentals=pix * cap * groups * depth,
        ),
    )(pixels, landmark_index, counts, factor)


def solution(mesh):
    placed = P(None, ("grp", "blk"))
    return jax.shard_map(
        functools.partial(per_device, mesh.shape["grp"], mesh.shape["blk"]),
        mesh=mesh,
        in_specs=(placed,) * 4,
        out_specs=(placed, placed),
        check_vma=False,
    )
```

```python
import functools

import jax
import jax.numpy as jnp
from jax import lax
from jax.experimental import pallas as pl
from jax.experimental.pallas import tpu as pltpu
from jax.sharding import PartitionSpec as P

MESH = pl.DeviceIdType.MESH
AUX = 16
CHUNK = 256
TOGETHER = 6
GIVE = 512


def three_way(value):
    high = value.astype(jnp.bfloat16)
    rest = value - high.astype(jnp.float32)
    mid = rest.astype(jnp.bfloat16)
    low = (rest - mid.astype(jnp.float32)).astype(jnp.bfloat16)
    return [part.astype(jnp.float32) for part in (high, mid, low)]


def kernel(
    groups, depth, pixels_in, index_in, counts_in, factor_in,
    scaled_ref, inv_ref, logdeg_ref,
    pixels_ref, index_ref, counts_ref, in_sem, out_sem,
    blocks, pix_aug, acc, rows_a, rows_b,
    recv_sem, z_sem, chip_sem, sib_sem, ra_send, ra_recv, rb_send, rb_recv,
):
    layers, pix = pixels_in.shape
    emb, cap = factor_in.shape
    chips = groups // 2
    g, z = lax.axis_index("grp"), lax.axis_index("blk")
    core, chip = lax.rem(g, 2), lax.div(g, 2)
    sib = g + 1 - 2 * core
    mine = blocks.at[chip * depth + z, core]

    loads = [
        pltpu.make_async_copy(src, dst, in_sem.at[at])
        for at, (src, dst) in enumerate(
            [
                (pixels_in, pixels_ref),
                (index_in, index_ref),
                (counts_in, counts_ref),
                (factor_in, mine.at[0:emb, :]),
            ]
        )
    ]
    for load in loads:
        load.start()

    barrier = pltpu.get_barrier_semaphore()

    def greet_group(k, carry):
        pl.semaphore_signal(
            barrier, inc=1, device_id=(lax.rem(g + k, groups), z), device_id_type=MESH
        )
        return carry

    def greet_depth(k, carry):
        pl.semaphore_signal(
            barrier, inc=1, device_id=(g, lax.rem(z + k, depth)), device_id_type=MESH
        )
        return carry

    lax.fori_loop(1, groups, greet_group, 0)
    lax.fori_loop(1, depth, greet_depth, 0)

    for load in loads:
        load.wait()

    pick = lax.broadcasted_iota(jnp.int32, (pix, cap), 0) == index_ref[...]
    land = jnp.dot(
        pixels_ref[...], pick.astype(jnp.bfloat16), preferred_element_type=jnp.float32
    )
    alive = lax.broadcasted_iota(jnp.int32, (1, cap), 1) < counts_ref[...]
    land_sq = jnp.where(alive, jnp.sum(land * land, axis=0, keepdims=True) * (-0.0625), -1e30)
    row = lax.broadcasted_iota(jnp.int32, (AUX, cap), 0)
    aux = jnp.where(row < 3, 1.0, 0.0)
    for at, part in enumerate(three_way(land_sq)):
        aux = jnp.where(row == 3 + at, part, aux)
    mine[emb : emb + AUX, :] = aux.astype(jnp.bfloat16)
    mine[emb + AUX : emb + AUX + layers, :] = land.astype(jnp.bfloat16)

    pl.semaphore_wait(barrier, groups + depth - 2)

    def send(slot, which, device, send_sem):
        ref = blocks.at[slot, which]
        return pltpu.make_async_remote_copy(
            src_ref=ref, dst_ref=ref, send_sem=send_sem, recv_sem=recv_sem.at[slot, which],
            device_id=device, device_id_type=MESH,
        )

    def slot_of(dc, dz):
        return lax.rem(chip + dc, chips) * depth + lax.rem(z + dz, depth)

    def to_depth(dz):
        return send(slot_of(0, 0), core, (g, lax.rem(z + dz, depth)), z_sem.at[dz])

    def to_chip(dz, dc):
        there = lax.rem(chip + dc, chips) * 2 + core
        return send(slot_of(0, dz), core, (there, z), chip_sem.at[dz, dc])

    def to_sib(dc, dz):
        return send(slot_of(dc, dz), core, (sib, z), sib_sem.at[dc, dz])

    def arrived(slot, which):
        send(slot, which, (sib, z), sib_sem.at[0, 0]).wait_recv()

    to_sib(0, 0).start()
    for dz in range(1, depth):
        to_depth(dz).start()
    for dc in range(1, chips):
        to_chip(0, dc).start()

    for at in range(0, pix, CHUNK):
        cols = pl.ds(at, CHUNK)
        own = pixels_ref[:, cols].astype(jnp.float32)
        pix_sq = jnp.sum(own * own, axis=0, keepdims=True) * (-0.0625)
        prow = lax.broadcasted_iota(jnp.int32, (AUX, CHUNK), 0)
        side = jnp.where((prow >= 3) & (prow < 6), 1.0, 0.0)
        for put, part in enumerate(three_way(pix_sq)):
            side = jnp.where(prow == put, part, side)
        pix_aug[0:AUX, cols] = side.astype(jnp.bfloat16)
        pix_aug[AUX : AUX + layers, cols] = (own * 0.125).astype(jnp.bfloat16)

    def absorb(held, first=False):
        fac = jnp.concatenate([blocks[slot, which, 0 : emb + AUX] for slot, which in held], axis=1)
        side = jnp.concatenate(
            [
                blocks[slot, which, emb : emb + AUX + layers].astype(jnp.float32).T
                for slot, which in held
            ],
            axis=0,
        ).astype(jnp.bfloat16)

        def exponent(at):
            return jnp.dot(
                side, pix_aug[:, at : at + CHUNK], preferred_element_type=jnp.float32
            )

        ahead = exponent(0)
        for at in range(0, pix, CHUNK):
            expo = ahead
            if at + CHUNK < pix:
                ahead = exponent(at + CHUNK)
            kern = jnp.exp(expo).astype(jnp.bfloat16)
            add = jnp.dot(fac, kern, preferred_element_type=jnp.float32)
            if first:
                acc[:, at : at + CHUNK] = add
            else:
                acc[:, at : at + CHUNK] += add

    def bunches(items):
        return [items[at : at + TOGETHER] for at in range(0, len(items), TOGETHER)]

    arrived(slot_of(0, 0), 1 - core)
    absorb([(slot_of(0, 0), 0), (slot_of(0, 0), 1)], first=True)

    def relay(dz, carry):
        slot = slot_of(0, dz)
        arrived(slot, core)
        for dc in range(1, chips):
            to_chip(dz, dc).start()
        to_sib(0, dz).start()
        return carry

    lax.fori_loop(1, depth, relay, 0)

    def near(dc, carry):
        slot = slot_of(dc, 0)
        arrived(slot, core)
        to_sib(dc, 0).start()
        return carry

    lax.fori_loop(1, chips, near, 0)

    early = [slot_of(0, dz) for dz in range(1, depth)] + [slot_of(dc, 0) for dc in range(1, chips)]
    for bunch in bunches(early):
        absorb([(slot, core) for slot in bunch])

    def pass_on(dz):
        for dc in range(1, chips):
            slot = slot_of(dc, dz)
            arrived(slot, core)
            to_sib(dc, dz).start()

    pass_on(1)
    for bunch in bunches(early):
        for slot in bunch:
            arrived(slot, 1 - core)
        absorb([(slot, 1 - core) for slot in bunch])

    def rest(dz, carry):
        @pl.when(dz + 1 < depth)
        def _():
            pass_on(dz + 1)

        row = [(slot_of(dc, dz), which) for dc in range(1, chips) for which in (core, 1 - core)]
        for bunch in bunches(row):
            for slot, which in bunch[1::2]:
                arrived(slot, which)
            absorb(bunch)
        return carry

    lax.fori_loop(1, depth, rest, 0)

    part = jnp.zeros((emb, 128), jnp.float32)
    for at in range(0, pix, 128):
        cols = pl.ds(at, 128)
        scaled = acc[0:emb, cols] * lax.rsqrt(acc[emb : emb + 1, cols])
        acc[0:emb, cols] = scaled
        part = part + scaled * scaled
    give_scaled = pltpu.make_async_copy(acc.at[0:emb, :], scaled_ref, out_sem)
    give_scaled.start()
    tall = jnp.concatenate([part, jnp.zeros((128 - emb, 128), jnp.float32)], axis=0)
    total = jnp.sum(tall.T, axis=0, keepdims=True)
    lane = lax.broadcasted_iota(jnp.int32, (1, 128), 1)
    total = jnp.where(lane == emb, counts_ref[...].astype(jnp.float32), total)

    def exchange(total, rows, count, device_of, send_sems, recv_sems):
        rows[0] = total

        def give(k):
            return pltpu.make_async_remote_copy(
                src_ref=rows.at[0], dst_ref=rows.at[k],
                send_sem=send_sems.at[k], recv_sem=recv_sems.at[k],
                device_id=device_of(k), device_id_type=MESH,
            )

        for k in range(1, count):
            give(k).start()
        for k in range(1, count):
            give(k).wait_recv()
            total = total + rows[k]
        for k in range(1, count):
            give(k).wait_send()
        return total

    total = exchange(total, rows_a, groups, lambda k: (lax.rem(g + k, groups), z), ra_send, ra_recv)
    total = exchange(total, rows_b, depth, lambda k: (g, lax.rem(z + k, depth)), rb_send, rb_recv)

    live = total[:, emb : emb + 1]
    logdeg_ref[...] = jnp.log(acc[emb : emb + 1, :] / live)
    inv = lax.rsqrt(total / (pix * groups * depth) + 1e-06)
    inv_ref[...] = jnp.broadcast_to(inv, (128, 128)).T[0:emb]

    give_scaled.wait()
    for dz in range(1, depth):
        to_depth(dz).wait_send()
    for dz in range(depth):
        for dc in range(1, chips):
            to_chip(dz, dc).wait_send()
    for dc in range(chips):
        for dz in range(depth):
            to_sib(dc, dz).wait_send()


def finish(scaled_in, inv_in, logdeg_in, emb_out, logdeg_out, held, inv_ref, in_sem, out_sem, sems):
    pix = scaled_in.shape[1]
    parts = [pl.ds(at, GIVE) for at in range(0, pix, GIVE)]
    direct = pltpu.make_async_copy(logdeg_in, logdeg_out, sems.at[0])
    norms = pltpu.make_async_copy(inv_in, inv_ref, sems.at[1])
    takes = [
        pltpu.make_async_copy(scaled_in.at[:, part], held.at[:, part], in_sem.at[at])
        for at, part in enumerate(parts)
    ]
    gives = [
        pltpu.make_async_copy(held.at[:, part], emb_out.at[:, part], out_sem.at[at])
        for at, part in enumerate(parts)
    ]
    norms.start()
    for take in takes:
        take.start()
    direct.start()
    norms.wait()
    for at, (take, give) in enumerate(zip(takes, gives)):
        take.wait()
        for col in range(at * GIVE, (at + 1) * GIVE, 128):
            held[:, col : col + 128] = held[:, col : col + 128] * inv_ref[...]
        give.start()
    direct.wait()
    for give in gives:
        give.wait()


def per_device(groups, depth, pixels, landmark_index, counts, factor):
    layers, pix = pixels.shape
    emb, cap = factor.shape
    chips = groups // 2
    vmem = pl.BlockSpec(memory_space=pltpu.VMEM)
    dma = pltpu.SemaphoreType.DMA
    scaled, inv, logdeg = pl.pallas_call(
        functools.partial(kernel, groups, depth),
        out_shape=(
            jax.ShapeDtypeStruct((emb, pix), jnp.float32),
            jax.ShapeDtypeStruct((emb, 128), jnp.float32),
            jax.ShapeDtypeStruct((1, pix), jnp.float32),
        ),
        in_specs=[pl.BlockSpec(memory_space=pltpu.HBM)] * 4,
        out_specs=(pl.BlockSpec(memory_space=pltpu.HBM), vmem, vmem),
        scratch_shapes=[
            pltpu.VMEM((layers, pix), jnp.bfloat16),
            pltpu.VMEM((1, cap), jnp.int32),
            pltpu.VMEM((1, 1), jnp.int32),
            dma((4,)),
            dma,
            pltpu.VMEM((chips * depth, 2, emb + AUX + layers, cap), jnp.bfloat16),
            pltpu.VMEM((AUX + layers, pix), jnp.bfloat16),
            pltpu.VMEM((emb + AUX, pix), jnp.float32),
            pltpu.VMEM((groups, 1, 128), jnp.float32),
            pltpu.VMEM((depth, 1, 128), jnp.float32),
            dma((chips * depth, 2)),
            dma((depth,)),
            dma((depth, chips)),
            dma((chips, depth)),
            dma((groups,)),
            dma((groups,)),
            dma((depth,)),
            dma((depth,)),
        ],
        compiler_params=pltpu.CompilerParams(
            collective_id=0, has_side_effects=True, vmem_limit_bytes=56 * 1024 * 1024
        ),
        cost_estimate=pl.CostEstimate(
            flops=2 * pix * cap * groups * depth * (emb + layers),
            bytes_accessed=4 * emb * pix,
            transcendentals=pix * cap * groups * depth,
        ),
    )(pixels, landmark_index, counts, factor)
    hbm = pl.BlockSpec(memory_space=pltpu.HBM)
    return pl.pallas_call(
        finish,
        out_shape=(
            jax.ShapeDtypeStruct((emb, pix), jnp.float32),
            jax.ShapeDtypeStruct((1, pix), jnp.float32),
        ),
        in_specs=[hbm] * 3,
        out_specs=(hbm, hbm),
        scratch_shapes=[
            pltpu.VMEM((emb, pix), jnp.float32),
            pltpu.VMEM((emb, 128), jnp.float32),
            dma((pix // GIVE,)),
            dma((pix // GIVE,)),
            dma((2,)),
        ],
        compiler_params=pltpu.CompilerParams(vmem_limit_bytes=56 * 1024 * 1024),
        cost_estimate=pl.CostEstimate(
            flops=emb * pix, bytes_accessed=8 * emb * pix, transcendentals=0
        ),
    )(scaled, inv, logdeg)


def solution(mesh):
    placed = P(None, ("grp", "blk"))
    return jax.shard_map(
        functools.partial(per_device, mesh.shape["grp"], mesh.shape["blk"]),
        mesh=mesh,
        in_specs=(placed,) * 4,
        out_specs=(placed, placed),
        check_vma=False,
    )
```
